32 devices in a mesh: row: 8 (over y, x, core), col: 4 (over z).
Axes of the slice: x: 2, y: 2, z: 4, core: 2. Of those that a mesh axis runs over, the one named last changes fastest.
Arguments:
- treated: bfloat16 [8192, 64], P('row'), may hold values from -6 to 6
- donors: bfloat16 [32768, 64], P('col'), may hold values from -6 to 6
- treated_counts: int32 [8192], P('row'), may hold values from 1 to 95, as said below
- donor_counts: int32 [32768], P('col'), may hold values from 1 to 95, as said below
Outputs:
- treated_dual: float32 [8192], P('row')
- donor_dual: float32 [32768], P('col')
The draws below stay inside these ranges and needn't reach their ends.
Inputs may be any that keep to these rules, and one draw needn't show every extreme that they name: `treated_counts`: positive region multiplicities. `donor_counts`: positive region multiplicities.
All inputs are finite; a program needn't handle non-finite values.
Results may differ from the reference program's by a relative error of at most 0.0003.
Values sent between devices are 32-bit elements; how exact they have to be, the bound alone decides.
A program may use at most 64 MiB of HBM per device.

```python
import jax
import jax.numpy as jnp
from jax import lax

DIM = 64
ITERS = 4
TREATED = 8192
DONORS = 32768


def region_counts(key, length):
    level_key, count_key = jax.random.split(key, 2)
    position = jnp.arange(length, dtype=jnp.int32)
    region = 32 * position // length
    shifts = jax.random.randint(level_key, (32,), 0, 4, dtype=jnp.int32)
    ladder = 32 + 63 * jnp.arange(32, dtype=jnp.int32) // 31
    capped = jnp.maximum(jnp.right_shift(ladder, shifts), 1)
    ceiling = jnp.take(capped, region)
    counts = jax.random.randint(count_key, (length,), 1, ceiling + 1, dtype=jnp.int32)
    counts = jnp.where(position == length - 1, 95, counts)
    counts = jnp.where(position == 0, 1, counts)
    return counts.astype(jnp.int32)


def embedded_points(key, amount):
    second_key = jax.random.fold_in(key, 1)
    values = jax.random.truncated_normal(second_key, -6.0, 6.0, (amount, DIM), jnp.float32)
    return values.astype(jnp.bfloat16)


def draw_treated(key, part):
    return embedded_points(jax.random.fold_in(key, 31), TREATED)


def draw_donors(key, part):
    return embedded_points(jax.random.fold_in(key, 47), DONORS)


def draw_treated_counts(key, part):
    return region_counts(jax.random.fold_in(key, 11), TREATED)


def draw_donor_counts(key, part):
    return region_counts(jax.random.fold_in(key, 23), DONORS)


def setup_inputs(seed: int = 0) -> dict:
    key_list = jax.random.split(jax.random.key(seed), 5)
    treated = draw_treated(jax.random.fold_in(key_list[4], 71), 0)
    donors = draw_donors(jax.random.fold_in(key_list[4], 71), 0)
    treated_counts = draw_treated_counts(jax.random.fold_in(key_list[4], 71), 0)
    donor_counts = draw_donor_counts(jax.random.fold_in(key_list[4], 71), 0)
    return dict(treated=treated, donors=donors, treated_counts=treated_counts, donor_counts=donor_counts)


entropic = 0.5


def soft_minimum(points, others, others_term):
    amount = points.shape[0]
    block_rows = min(amount, 512)
    others_sq = jnp.sum(jnp.square(others.astype(jnp.float32)), axis=1)

    def one_block(pieces):
        products = jnp.dot(pieces, others.T, preferred_element_type=jnp.float32)
        own_sq = jnp.sum(jnp.square(pieces.astype(jnp.float32)), axis=1)
        distance = own_sq[:, None] + others_sq[None, :] - 2.0 * products
        scores = (others_term[None, :] - distance) / entropic
        highest = jnp.max(scores, axis=1)
        summed = jnp.sum(jnp.exp(scores - highest[:, None]), axis=1)
        return -entropic * (highest + jnp.log(summed))

    blocks = points.reshape(amount // block_rows, block_rows, points.shape[1])
    return lax.map(one_block, blocks).reshape(amount)


def reference(treated, donors, treated_counts, donor_counts):
    treated_float = treated_counts.astype(jnp.float32)
    donor_float = donor_counts.astype(jnp.float32)
    treated_log = jnp.log(treated_float) - jnp.log(jnp.sum(treated_float))
    donor_log = jnp.log(donor_float) - jnp.log(jnp.sum(donor_float))
    donor_dual = jnp.zeros((donors.shape[0],), jnp.float32)
    treated_dual = jnp.zeros((treated.shape[0],), jnp.float32)
    for sweep in range(ITERS):
        treated_dual = soft_minimum(treated, donors, donor_dual + entropic * donor_log)
        donor_dual = soft_minimum(donors, treated, treated_dual + entropic * treated_log)
    return treated_dual, donor_dual
```

```python
import functools
import math

import jax
import jax.numpy as jnp
from jax import lax
from jax.experimental import pallas as pl
from jax.experimental.pallas import tpu as pltpu
from jax.sharding import PartitionSpec as P

ITERS = 4
LOG2E = math.log2(math.e)
LN2 = math.log(2.0)
CH = 1024
LN = 128
KS = CH // LN
RB = 256
RV = 128
SHIFT = 20.0
MESH = pl.DeviceIdType.MESH
F32 = jnp.float32
BF16 = jnp.bfloat16


def split3(v):
    a = v.astype(BF16).astype(F32)
    r = v - a
    b = r.astype(BF16).astype(F32)
    return a, b, r - b


def kernel(nr, nc, x_ref, y_ref, tc_ref, dc_ref, f_ref, g_ref,
           xa, yt, e_ref, gam, m_ref, s_ref, om, q_ref, p_ref, u_ref, ysq, xsq,
           rbuf, cbuf, nbuf, mbuf, rs, rr, cs, cr, ns, nrv, ms, mr):
    rows = x_ref.shape[0]
    cols = y_ref.shape[0]
    dim = x_ref.shape[1]
    nch = cols // CH
    nrb = rows // RB
    rl = rows // LN
    me_r = lax.axis_index("row")
    me_c = lax.axis_index("col")
    row_peers = [lax.rem(me_r + d, nr) for d in range(1, nr)]
    col_peers = [lax.rem(me_c + d, nc) for d in range(1, nc)]

    barrier = pltpu.get_barrier_semaphore()
    for p in row_peers:
        pl.semaphore_signal(barrier, inc=1, device_id={"row": p}, device_id_type=MESH)
    for p in col_peers:
        pl.semaphore_signal(barrier, inc=1, device_id={"col": p}, device_id_type=MESH)

    def to_col(ref_at, send, recv):
        out = []
        for d, p in enumerate(col_peers):
            out.append(pltpu.make_async_remote_copy(
                src_ref=ref_at, dst_ref=ref_at, send_sem=send(d), recv_sem=recv(d),
                device_id={"col": p}, device_id_type=MESH))
        return out

    def to_row(ref_at, send, recv):
        out = []
        for d, p in enumerate(row_peers):
            out.append(pltpu.make_async_remote_copy(
                src_ref=ref_at, dst_ref=ref_at, send_sem=send(d), recv_sem=recv(d),
                device_id={"row": p}, device_id_type=MESH))
        return out

    tcf = tc_ref[...].astype(F32)
    dcf = dc_ref[...].astype(F32)
    xf = x_ref[...].astype(F32)
    c = xf * (4.0 * LOG2E)
    c1, c2, c3 = split3(c)
    ri = lax.broadcasted_iota(jnp.int32, (dim, 4 * dim), 0)
    ci = lax.broadcasted_iota(jnp.int32, (dim, 4 * dim), 1)
    wide = jnp.zeros((rows, 4 * dim), F32)
    for k, part in enumerate((c1, c2, c3)):
        place = (ri + k * dim == ci).astype(BF16)
        wide = wide + jnp.dot(part.astype(BF16), place, preferred_element_type=F32)
    lane = lax.broadcasted_iota(jnp.int32, (rows, 4 * dim), 1)
    wide = jnp.where((lane >= 3 * dim) & (lane < 3 * dim + 3), 1.0, wide)
    xa[...] = wide.astype(BF16)
    sq = jnp.broadcast_to(jnp.sum(xf * xf, axis=1, keepdims=True), (rows, LN))
    for r in range(rl):
        xsq[r:r + 1, :] = sq[r * LN:(r + 1) * LN, :].T[0:1, :]

    k1 = lax.broadcasted_iota(jnp.int32, (3 * dim, dim), 0)
    k2 = lax.broadcasted_iota(jnp.int32, (3 * dim, dim), 1)
    stack = (lax.rem(k1, dim) == k2).astype(BF16)

    def put_q(ch, q8):
        row = jnp.concatenate([q8[k:k + 1, :] for k in range(KS)], axis=1)
        a, b, cc = split3(row)
        r16 = lax.broadcasted_iota(jnp.int32, (16, CH), 0)
        val = jnp.where(r16 == 0, a, jnp.where(r16 == 1, b, jnp.where(r16 == 2, cc, jnp.where(r16 < 6, 1.0, 0.0))))
        yt[3 * dim:3 * dim + 16, pl.ds(pl.multiple_of(ch * CH, CH), CH)] = val.astype(BF16)

    def prep(ch, carry):
        js = pl.ds(pl.multiple_of(ch * CH, CH), CH)
        r8 = pl.ds(pl.multiple_of(ch * KS, KS), KS)
        t = lax.dot_general(stack, y_ref[js, :], (((1,), (1,)), ((), ())), preferred_element_type=F32)
        yt[0:3 * dim, js] = t.astype(BF16)
        yt[3 * dim + 16:4 * dim, js] = jnp.zeros((dim - 16, CH), BF16)
        t1 = t[0:dim, :]
        n2 = jnp.sum(t1 * t1, axis=0, keepdims=True)
        n8 = jnp.concatenate([n2[:, k * LN:(k + 1) * LN] for k in range(KS)], axis=0)
        ysq[r8, :] = n8
        q8 = jnp.log2(dc_ref[r8, :].astype(F32)) - (2.0 * LOG2E) * n8
        q_ref[r8, :] = q8
        put_q(ch, q8)
        return carry

    lax.fori_loop(0, nch, prep, 0)

    tsum = tcf[0:8, :]
    for r in range(1, rl // 8):
        tsum = tsum + tcf[r * 8:(r + 1) * 8, :]
    dsum = dcf[0:8, :]
    for r in range(1, cols // LN // 8):
        dsum = dsum + dcf[r * 8:(r + 1) * 8, :]
    mbuf[me_r] = tsum
    nbuf[me_c] = dsum

    pl.semaphore_wait(barrier, nr + nc - 2)
    n_copies = to_col(nbuf.at[me_c], lambda d: ns.at[d], lambda d: nrv.at[d])
    m_copies = to_row(mbuf.at[me_r], lambda d: ms.at[d], lambda d: mr.at[d])
    for cp in n_copies + m_copies:
        cp.start()

    def group(v, k):
        return v[:, k * LN:(k + 1) * LN]

    def score_rows(keep):
        m_ref[...] = jnp.full(m_ref.shape, -jnp.inf, F32)
        s_ref[...] = jnp.zeros(s_ref.shape, F32)

        def tile(step, carry):
            ch = step // nrb
            rb = step % nrb
            js = pl.ds(pl.multiple_of(ch * CH, CH), CH)
            rs_ = pl.ds(pl.multiple_of(rb * RB, RB), RB)
            sc = jnp.dot(xa[rs_, :], yt[:, js], preferred_element_type=F32)
            top = group(sc, 0)
            for k in range(1, KS):
                top = jnp.maximum(top, group(sc, k))
            old = m_ref[rs_, :]
            new = jnp.maximum(old, top)
            if keep:
                low = new - SHIFT
                gam[rs_, pl.ds(pl.multiple_of(ch * LN, LN), LN)] = new
            else:
                low = new
            tot = None
            for k in range(KS):
                ex = jnp.exp2(group(sc, k) - low)
                if keep:
                    e_ref[rs_, pl.ds(pl.multiple_of(ch * CH + k * LN, LN), LN)] = ex
                tot = ex if tot is None else tot + ex
            s_ref[rs_, :] = s_ref[rs_, :] * jnp.exp2(old - new) + tot
            m_ref[rs_, :] = new
            return carry

        lax.fori_loop(0, nch * nrb, tile, 0)

    def rows_dense_lse(it):
        for r in range(rl):
            mt = m_ref[r * LN:(r + 1) * LN, :].T
            st = s_ref[r * LN:(r + 1) * LN, :].T
            top = jnp.max(mt, axis=0, keepdims=True)
            tot = jnp.sum(st * jnp.exp2(mt - top), axis=0, keepdims=True)
            rbuf[it, me_c, r:r + 1, :] = top + jnp.log2(tot)

    def row_exchange(it):
        copies = to_col(rbuf.at[it, me_c], lambda d: rs.at[it, d], lambda d: rr.at[it, d])
        for cp in copies:
            cp.start()
        for cp in copies:
            cp.wait()

    def spread(v, r):
        return jnp.broadcast_to(v[r:r + 1, :], (LN, LN)).T

    def lse_merge(get, n):
        top = get(0)
        for k in range(1, n):
            top = jnp.maximum(top, get(k))
        tot = jnp.exp2(get(0) - top)
        for k in range(1, n):
            tot = tot + jnp.exp2(get(k) - top)
        return top + jnp.log2(tot)

    def sum_merge(get, n):
        tot = get(0)
        for k in range(1, n):
            tot = tot + get(k)
        return tot

    def send_cols(it, ch):
        part = cbuf.at[it, me_r, pl.ds(pl.multiple_of(ch * KS, KS), KS)]
        for cp in to_row(part, lambda d: cs.at[it, ch, d], lambda d: cr.at[it, ch, d]):
            cp.start()

    def wait_cols(it):
        def one(ch, carry):
            part = cbuf.at[it, me_r, pl.ds(pl.multiple_of(ch * KS, KS), KS)]
            for cp in to_row(part, lambda d: cs.at[it, ch, d], lambda d: cr.at[it, ch, d]):
                cp.wait()
            return carry
        lax.fori_loop(0, nch, one, 0)

    score_rows(False)
    rows_dense_lse(0)
    row_exchange(0)
    lsum = lse_merge(lambda k: rbuf[0, k], nc)
    p = jnp.log2(tcf) - lsum
    p_ref[...] = p
    l128 = lax.broadcasted_iota(jnp.int32, (LN, 2 * dim), 1)
    for r in range(rl):
        a, b, cc = split3(spread(p, r))
        half = xa[r * LN:(r + 1) * LN, 2 * dim:4 * dim].astype(F32)
        half = jnp.where(l128 == dim + 3, a, jnp.where(l128 == dim + 4, b, jnp.where(l128 == dim + 5, cc, half)))
        xa[r * LN:(r + 1) * LN, 2 * dim:4 * dim] = half.astype(BF16)

    def col_chunk(ch, carry):
        js = pl.ds(pl.multiple_of(ch * CH, CH), CH)

        def tile(rb, ms_):
            old, tot = ms_
            rs_ = pl.ds(pl.multiple_of(rb * RB, RB), RB)
            sc = jnp.dot(xa[rs_, :], yt[:, js], preferred_element_type=F32)
            sc = sc.reshape(RB // 8, 8, CH)
            new = jnp.maximum(old, jnp.max(sc, axis=0))
            ex = jnp.sum(jnp.exp2(sc - new[None]), axis=0)
            return new, tot * jnp.exp2(old - new) + ex

        top, tot = lax.fori_loop(
            0, nrb, tile, (jnp.full((8, CH), -jnp.inf, F32), jnp.zeros((8, CH), F32)))
        best = jnp.max(top, axis=0, keepdims=True)
        tot = jnp.sum(tot * jnp.exp2(top - best), axis=0, keepdims=True)
        val = best + jnp.log2(tot)
        cbuf[0, me_r, pl.ds(pl.multiple_of(ch * KS, KS), KS), :] = jnp.concatenate(
            [group(val, k) for k in range(KS)], axis=0)
        send_cols(0, ch)
        return carry

    lax.fori_loop(0, nch, col_chunk, 0)
    wait_cols(0)

    def new_q(ch, carry):
        r8 = pl.ds(pl.multiple_of(ch * KS, KS), KS)
        total = lse_merge(lambda k: cbuf[0, k, r8, :], nr)
        q8 = jnp.log2(dc_ref[r8, :].astype(F32)) + (q_ref[r8, :] - total)
        q_ref[r8, :] = q8
        put_q(ch, q8)
        return carry

    lax.fori_loop(0, nch, new_q, 0)

    score_rows(True)
    rows_dense_lse(1)
    row_exchange(1)
    lsum = lse_merge(lambda k: rbuf[1, k], nc) - SHIFT
    p_ref[...] = p_ref[...] - lsum
    for r in range(rl):
        rsl = slice(r * LN, (r + 1) * LN)
        lb = spread(lsum, r)
        for ch in range(nch):
            gam[rsl, ch * LN:(ch + 1) * LN] = jnp.exp2(gam[rsl, ch * LN:(ch + 1) * LN] + (SHIFT - lb))
        om[rsl, :] = spread(tcf, r)

    def sum_cols(it):
        def chunk(ch, carry):
            def tile(rv, acc):
                rs_ = pl.ds(pl.multiple_of(rv * RV, RV), RV)
                w = gam[rs_, pl.ds(pl.multiple_of(ch * LN, LN), LN)] * om[rs_, :]
                out = []
                for k in range(KS):
                    ex = e_ref[rs_, pl.ds(pl.multiple_of(ch * CH + k * LN, LN), LN)]
                    out.append(acc[k] + jnp.sum((ex * w).reshape(RV // 8, 8, LN), axis=0))
                return tuple(out)

            acc = lax.fori_loop(0, rows // RV, tile, tuple(jnp.zeros((8, LN), F32) for _ in range(KS)))
            val = jnp.concatenate([jnp.sum(a, axis=0, keepdims=True) for a in acc], axis=0)
            cbuf[it, me_r, pl.ds(pl.multiple_of(ch * KS, KS), KS), :] = val * (2.0 ** (-2 * SHIFT))
            send_cols(it, ch)
            return carry

        lax.fori_loop(0, nch, chunk, 0)
        wait_cols(it)
        return sum_merge(lambda k: cbuf[it, k], nr)

    def sum_rows(it):
        s_ref[...] = jnp.zeros(s_ref.shape, F32)

        def chunk(ch, carry):
            u8 = u_ref[pl.ds(pl.multiple_of(ch * KS, KS), KS), :]

            def tile(rv, carry2):
                rs_ = pl.ds(pl.multiple_of(rv * RV, RV), RV)
                tot = None
                for k in range(KS):
                    ex = e_ref[rs_, pl.ds(pl.multiple_of(ch * CH + k * LN, LN), LN)] * u8[k:k + 1, :]
                    tot = ex if tot is None else tot + ex
                s_ref[rs_, :] += tot * gam[rs_, pl.ds(pl.multiple_of(ch * LN, LN), LN)]
                return carry2

            return lax.fori_loop(0, rows // RV, tile, carry)

        lax.fori_loop(0, nch, chunk, 0)
        for r in range(rl):
            st = s_ref[r * LN:(r + 1) * LN, :].T
            rbuf[it, me_c, r:r + 1, :] = jnp.sum(st, axis=0, keepdims=True) * (2.0 ** (-2 * SHIFT))
        row_exchange(it)
        return sum_merge(lambda k: rbuf[it, k], nc)

    total = sum_cols(1)
    rsum = None
    for it in range(2, ITERS):
        u_ref[...] = dcf / total
        rsum = sum_rows(it)
        omega = tcf / rsum
        for r in range(rl):
            om[r * LN:(r + 1) * LN, :] = spread(omega, r)
        total = sum_cols(it)

    for cp in n_copies + m_copies:
        cp.wait()
    mall = jnp.log2(jnp.sum(sum_merge(lambda k: mbuf[k], nr), keepdims=True))
    nall = jnp.log2(jnp.sum(sum_merge(lambda k: nbuf[k], nc), keepdims=True))
    f_ref[...] = (0.5 * LN2) * (
        p_ref[...] - jnp.log2(rsum) + ITERS * nall - (ITERS - 1) * mall) + xsq[...]
    g_ref[...] = (0.5 * LN2) * (
        q_ref[...] - jnp.log2(total) + ITERS * (mall - nall)) + ysq[...]


def on_device(nr, nc, treated, donors, treated_counts, donor_counts):
    rows, dim = treated.shape
    cols = donors.shape[0]
    rl, cl, nch = rows // LN, cols // LN, cols // CH
    vm = pltpu.VMEM
    dma = pltpu.SemaphoreType.DMA
    f, g = pl.pallas_call(
        functools.partial(kernel, nr, nc),
        out_shape=(jax.ShapeDtypeStruct((rl, LN), F32), jax.ShapeDtypeStruct((cl, LN), F32)),
        in_specs=[pl.BlockSpec(memory_space=vm)] * 4,
        out_specs=(pl.BlockSpec(memory_space=vm), pl.BlockSpec(memory_space=vm)),
        scratch_shapes=[
            vm((rows, 4 * dim), BF16),
            vm((4 * dim, cols), BF16),
            vm((rows, cols), F32),
            vm((rows, nch * LN), F32),
            vm((rows, LN), F32),
            vm((rows, LN), F32),
            vm((rows, LN), F32),
            vm((cl, LN), F32),
            vm((rl, LN), F32),
            vm((cl, LN), F32),
            vm((cl, LN), F32),
            vm((rl, LN), F32),
            vm((ITERS, nc, rl, LN), F32),
            vm((ITERS, nr, cl, LN), F32),
            vm((nc, 8, LN), F32),
            vm((nr, 8, LN), F32),
            dma((ITERS, nc - 1)), dma((ITERS, nc - 1)),
            dma((ITERS, nch, nr - 1)), dma((ITERS, nch, nr - 1)),
            dma((nc - 1,)), dma((nc - 1,)),
            dma((nr - 1,)), dma((nr - 1,)),
        ],
        compiler_params=pltpu.CompilerParams(
            collective_id=0, has_side_effects=True, vmem_limit_bytes=60 * 1024 * 1024),
    )(treated, donors, treated_counts.reshape(rl, LN), donor_counts.reshape(cl, LN))
    return f.reshape(rows), g.reshape(cols)


def solution(mesh):
    in_specs = (P("row", None), P("col", None), P("row"), P("col"))
    out_specs = (P("row"), P("col"))
    return jax.shard_map(
        functools.partial(on_device, mesh.shape["row"], mesh.shape["col"]),
        mesh=mesh, in_specs=in_specs, out_specs=out_specs, check_vma=False,
    )
```

```python
import functools
import math

import jax
import jax.numpy as jnp
from jax import lax
from jax.experimental import pallas as pl
from jax.experimental.pallas import tpu as pltpu
from jax.sharding import PartitionSpec as P

ITERS = 4
LOG2E = math.log2(math.e)
LN2 = math.log(2.0)
CH = 1024
LN = 128
KS = CH // LN
RB = 256
RV = 128
SHIFT = 20.0
UR = 4
UC = 4
US = 8
MESH = pl.DeviceIdType.MESH
F32 = jnp.float32
BF16 = jnp.bfloat16


def split3(v):
    a = v.astype(BF16).astype(F32)
    r = v - a
    b = r.astype(BF16).astype(F32)
    return a, b, r - b


def kernel(nr, nc, x_ref, y_ref, tc_ref, dc_ref, f_ref, g_ref,
           xa, yt, e_ref, gam, m_ref, s_ref, om, q_ref, p_ref, u_ref, ysq, xsq,
           rbuf, cbuf, nbuf, mbuf, rs, rr, cs, cr, ns, nrv, ms, mr):
    dim, rows = x_ref.shape
    cols = y_ref.shape[1]
    nch = cols // CH
    nrb = rows // RB
    rl = rows // LN
    me_r = lax.axis_index("row")
    me_c = lax.axis_index("col")
    row_peers = [lax.rem(me_r + d, nr) for d in range(1, nr)]
    col_peers = [lax.rem(me_c + d, nc) for d in range(1, nc)]

    barrier = pltpu.get_barrier_semaphore()
    for p in row_peers:
        pl.semaphore_signal(barrier, inc=1, device_id={"row": p}, device_id_type=MESH)
    for p in col_peers:
        pl.semaphore_signal(barrier, inc=1, device_id={"col": p}, device_id_type=MESH)

    def to_col(ref_at, send, recv):
        out = []
        for d, p in enumerate(col_peers):
            out.append(pltpu.make_async_remote_copy(
                src_ref=ref_at, dst_ref=ref_at, send_sem=send(d), recv_sem=recv(d),
                device_id={"col": p}, device_id_type=MESH))
        return out

    def to_row(ref_at, send, recv):
        out = []
        for d, p in enumerate(row_peers):
            out.append(pltpu.make_async_remote_copy(
                src_ref=ref_at, dst_ref=ref_at, send_sem=send(d), recv_sem=recv(d),
                device_id={"row": p}, device_id_type=MESH))
        return out

    tcf = tc_ref[...].astype(F32)
    dcf = dc_ref[...].astype(F32)
    xf = x_ref[...].astype(F32)
    c = xf * (4.0 * LOG2E)
    c1, c2, c3 = split3(c)
    ri = lax.broadcasted_iota(jnp.int32, (dim, 4 * dim), 0)
    ci = lax.broadcasted_iota(jnp.int32, (dim, 4 * dim), 1)
    wide = jnp.zeros((rows, 4 * dim), F32)
    for k, part in enumerate((c1, c2, c3)):
        place = (ri + k * dim == ci).astype(BF16)
        wide = wide + lax.dot_general(
            part.astype(BF16), place, (((0,), (0,)), ((), ())), preferred_element_type=F32)
    lane = lax.broadcasted_iota(jnp.int32, (rows, 4 * dim), 1)
    wide = jnp.where((lane >= 3 * dim) & (lane < 3 * dim + 3), 1.0, wide)
    xa[...] = wide.astype(BF16)
    sq = jnp.sum(xf * xf, axis=0, keepdims=True)
    for r in range(rl):
        xsq[r:r + 1, :] = sq[:, r * LN:(r + 1) * LN]

    def put_q(ch, q8):
        row = jnp.concatenate([q8[k:k + 1, :] for k in range(KS)], axis=1)
        a, b, cc = split3(row)
        r16 = lax.broadcasted_iota(jnp.int32, (16, CH), 0)
        val = jnp.where(r16 == 0, a, jnp.where(r16 == 1, b, jnp.where(r16 == 2, cc, jnp.where(r16 < 6, 1.0, 0.0))))
        yt[3 * dim:3 * dim + 16, pl.ds(pl.multiple_of(ch * CH, CH), CH)] = val.astype(BF16)

    def prep(ch, carry):
        js = pl.ds(pl.multiple_of(ch * CH, CH), CH)
        r8 = pl.ds(pl.multiple_of(ch * KS, KS), KS)
        yc = y_ref[:, js]
        for k in range(3):
            yt[k * dim:(k + 1) * dim, js] = yc
        yt[3 * dim + 16:4 * dim, js] = jnp.zeros((dim - 16, CH), BF16)
        t1 = yc.astype(F32)
        n2 = jnp.sum(t1 * t1, axis=0, keepdims=True)
        n8 = jnp.concatenate([n2[:, k * LN:(k + 1) * LN] for k in range(KS)], axis=0)
        ysq[r8, :] = n8
        q8 = jnp.log2(dc_ref[r8, :].astype(F32)) - (2.0 * LOG2E) * n8
        q_ref[r8, :] = q8
        put_q(ch, q8)
        return carry

    lax.fori_loop(0, nch, prep, 0)

    tsum = tcf[0:8, :]
    for r in range(1, rl // 8):
        tsum = tsum + tcf[r * 8:(r + 1) * 8, :]
    dsum = dcf[0:8, :]
    for r in range(1, cols // LN // 8):
        dsum = dsum + dcf[r * 8:(r + 1) * 8, :]
    mbuf[me_r] = tsum
    nbuf[me_c] = dsum

    pl.semaphore_wait(barrier, nr + nc - 2)
    n_copies = to_col(nbuf.at[me_c], lambda d: ns.at[d], lambda d: nrv.at[d])
    m_copies = to_row(mbuf.at[me_r], lambda d: ms.at[d], lambda d: mr.at[d])
    for cp in n_copies + m_copies:
        cp.start()

    def group(v, k):
        return v[:, k * LN:(k + 1) * LN]

    def score_rows(keep):
        m_ref[...] = jnp.full(m_ref.shape, -jnp.inf, F32)
        s_ref[...] = jnp.zeros(s_ref.shape, F32)

        def tile(step, carry):
            ch = step // nrb
            rb = step % nrb
            js = pl.ds(pl.multiple_of(ch * CH, CH), CH)
            rs_ = pl.ds(pl.multiple_of(rb * RB, RB), RB)
            sc = jnp.dot(xa[rs_, :], yt[:, js], preferred_element_type=F32)
            top = group(sc, 0)
            for k in range(1, KS):
                top = jnp.maximum(top, group(sc, k))
            old = m_ref[rs_, :]
            new = jnp.maximum(old, top)
            if keep:
                low = new - SHIFT
                gam[rs_, pl.ds(pl.multiple_of(ch * LN, LN), LN)] = new
            else:
                low = new
            tot = None
            for k in range(KS):
                ex = jnp.exp2(group(sc, k) - low)
                if keep:
                    e_ref[rs_, pl.ds(pl.multiple_of(ch * CH + k * LN, LN), LN)] = ex
                tot = ex if tot is None else tot + ex
            s_ref[rs_, :] = s_ref[rs_, :] * jnp.exp2(old - new) + tot
            m_ref[rs_, :] = new
            return carry

        lax.fori_loop(0, nch * nrb, tile, 0, unroll=UR)

    def rows_dense_lse(it):
        for r in range(rl):
            mt = m_ref[r * LN:(r + 1) * LN, :].T
            st = s_ref[r * LN:(r + 1) * LN, :].T
            top = jnp.max(mt, axis=0, keepdims=True)
            tot = jnp.sum(st * jnp.exp2(mt - top), axis=0, keepdims=True)
            rbuf[it, me_c, r:r + 1, :] = top + jnp.log2(tot)

    def row_exchange(it):
        copies = to_col(rbuf.at[it, me_c], lambda d: rs.at[it, d], lambda d: rr.at[it, d])
        for cp in copies:
            cp.start()
        for cp in copies:
            cp.wait()

    def spread(v, r):
        return jnp.broadcast_to(v[r:r + 1, :], (LN, LN)).T

    def lse_merge(get, n):
        top = get(0)
        for k in range(1, n):
            top = jnp.maximum(top, get(k))
        tot = jnp.exp2(get(0) - top)
        for k in range(1, n):
            tot = tot + jnp.exp2(get(k) - top)
        return top + jnp.log2(tot)

    def sum_merge(get, n):
        tot = get(0)
        for k in range(1, n):
            tot = tot + get(k)
        return tot

    cuts = (0, nch * 3 // 4, nch)

    def col_copies(it, n):
        part = cbuf.at[it, me_r, cuts[n] * KS:cuts[n + 1] * KS]
        return to_row(part, lambda d: cs.at[it, n, d], lambda d: cr.at[it, n, d])

    def over_chunks(it, chunk):
        for n in range(2):
            lax.fori_loop(cuts[n], cuts[n + 1], chunk, 0)
            for cp in col_copies(it, n):
                cp.start()
        for n in range(2):
            for cp in col_copies(it, n):
                cp.wait()

    score_rows(False)
    rows_dense_lse(0)
    row_exchange(0)
    lsum = lse_merge(lambda k: rbuf[0, k], nc)
    p = jnp.log2(tcf) - lsum
    p_ref[...] = p
    l128 = lax.broadcasted_iota(jnp.int32, (LN, 2 * dim), 1)
    for r in range(rl):
        a, b, cc = split3(spread(p, r))
        half = xa[r * LN:(r + 1) * LN, 2 * dim:4 * dim].astype(F32)
        half = jnp.where(l128 == dim + 3, a, jnp.where(l128 == dim + 4, b, jnp.where(l128 == dim + 5, cc, half)))
        xa[r * LN:(r + 1) * LN, 2 * dim:4 * dim] = half.astype(BF16)

    def col_chunk(ch, carry):
        js = pl.ds(pl.multiple_of(ch * CH, CH), CH)

        def tile(rb, ms_):
            old, tot = ms_
            rs_ = pl.ds(pl.multiple_of(rb * RB, RB), RB)
            sc = jnp.dot(xa[rs_, :], yt[:, js], preferred_element_type=F32)
            sc = sc.reshape(RB // 8, 8, CH)
            new = jnp.maximum(old, jnp.max(sc, axis=0))
            ex = jnp.sum(jnp.exp2(sc - new[None]), axis=0)
            return new, tot * jnp.exp2(old - new) + ex

        top, tot = lax.fori_loop(
            0, nrb, tile, (jnp.full((8, CH), -jnp.inf, F32), jnp.zeros((8, CH), F32)), unroll=UC)
        best = jnp.max(top, axis=0, keepdims=True)
        tot = jnp.sum(tot * jnp.exp2(top - best), axis=0, keepdims=True)
        val = best + jnp.log2(tot)
        cbuf[0, me_r, pl.ds(pl.multiple_of(ch * KS, KS), KS), :] = jnp.concatenate(
            [group(val, k) for k in range(KS)], axis=0)
        return carry

    over_chunks(0, col_chunk)

    def new_q(ch, carry):
        r8 = pl.ds(pl.multiple_of(ch * KS, KS), KS)
        total = lse_merge(lambda k: cbuf[0, k, r8, :], nr)
        q8 = jnp.log2(dc_ref[r8, :].astype(F32)) + (q_ref[r8, :] - total)
        q_ref[r8, :] = q8
        put_q(ch, q8)
        return carry

    lax.fori_loop(0, nch, new_q, 0)

    score_rows(True)
    rows_dense_lse(1)
    row_exchange(1)
    lsum = lse_merge(lambda k: rbuf[1, k], nc) - SHIFT
    p_ref[...] = p_ref[...] - lsum
    for r in range(rl):
        rsl = slice(r * LN, (r + 1) * LN)
        lb = spread(lsum, r)
        for ch in range(nch):
            gam[rsl, ch * LN:(ch + 1) * LN] = jnp.exp2(gam[rsl, ch * LN:(ch + 1) * LN] + (SHIFT - lb))
        om[rsl, :] = spread(tcf, r)

    def sum_cols(it):
        def chunk(ch, carry):
            def tile(rv, acc):
                rs_ = pl.ds(pl.multiple_of(rv * RV, RV), RV)
                w = gam[rs_, pl.ds(pl.multiple_of(ch * LN, LN), LN)] * om[rs_, :]
                out = []
                for k in range(KS):
                    ex = e_ref[rs_, pl.ds(pl.multiple_of(ch * CH + k * LN, LN), LN)]
                    out.append(acc[k] + jnp.sum((ex * w).reshape(RV // 8, 8, LN), axis=0))
                return tuple(out)

            acc = lax.fori_loop(0, rows // RV, tile, tuple(jnp.zeros((8, LN), F32) for _ in range(KS)), unroll=US)
            val = jnp.concatenate([jnp.sum(a, axis=0, keepdims=True) for a in acc], axis=0)
            cbuf[it, me_r, pl.ds(pl.multiple_of(ch * KS, KS), KS), :] = val * (2.0 ** (-2 * SHIFT))
            return carry

        over_chunks(it, chunk)
        return sum_merge(lambda k: cbuf[it, k], nr)

    def sum_rows(it):
        s_ref[...] = jnp.zeros(s_ref.shape, F32)

        def chunk(ch, carry):
            u8 = u_ref[pl.ds(pl.multiple_of(ch * KS, KS), KS), :]

            def tile(rv, carry2):
                rs_ = pl.ds(pl.multiple_of(rv * RV, RV), RV)
                tot = None
                for k in range(KS):
                    ex = e_ref[rs_, pl.ds(pl.multiple_of(ch * CH + k * LN, LN), LN)] * u8[k:k + 1, :]
                    tot = ex if tot is None else tot + ex
                s_ref[rs_, :] += tot * gam[rs_, pl.ds(pl.multiple_of(ch * LN, LN), LN)]
                return carry2

            return lax.fori_loop(0, rows // RV, tile, carry, unroll=US)

        lax.fori_loop(0, nch, chunk, 0)
        for r in range(rl):
            st = s_ref[r * LN:(r + 1) * LN, :].T
            rbuf[it, me_c, r:r + 1, :] = jnp.sum(st, axis=0, keepdims=True) * (2.0 ** (-2 * SHIFT))
        row_exchange(it)
        return sum_merge(lambda k: rbuf[it, k], nc)

    total = sum_cols(1)
    rsum = None
    for it in range(2, ITERS):
        u_ref[...] = dcf / total
        rsum = sum_rows(it)
        omega = tcf / rsum
        for r in range(rl):
            om[r * LN:(r + 1) * LN, :] = spread(omega, r)
        total = sum_cols(it)

    for cp in n_copies + m_copies:
        cp.wait()
    mall = jnp.log2(jnp.sum(sum_merge(lambda k: mbuf[k], nr), keepdims=True))
    nall = jnp.log2(jnp.sum(sum_merge(lambda k: nbuf[k], nc), keepdims=True))
    f_ref[...] = (0.5 * LN2) * (
        p_ref[...] - jnp.log2(rsum) + ITERS * nall - (ITERS - 1) * mall) + xsq[...]
    g_ref[...] = (0.5 * LN2) * (
        q_ref[...] - jnp.log2(total) + ITERS * (mall - nall)) + ysq[...]


def on_device(nr, nc, treated, donors, treated_counts, donor_counts):
    rows, dim = treated.shape
    cols = donors.shape[0]
    rl, cl, nch = rows // LN, cols // LN, cols // CH
    vm = pltpu.VMEM
    dma = pltpu.SemaphoreType.DMA
    f, g = pl.pallas_call(
        functools.partial(kernel, nr, nc),
        out_shape=(jax.ShapeDtypeStruct((rl, LN), F32), jax.ShapeDtypeStruct((cl, LN), F32)),
        in_specs=[pl.BlockSpec(memory_space=vm)] * 4,
        out_specs=(pl.BlockSpec(memory_space=vm), pl.BlockSpec(memory_space=vm)),
        scratch_shapes=[
            vm((rows, 4 * dim), BF16),
            vm((4 * dim, cols), BF16),
            vm((rows, cols), F32),
            vm((rows, nch * LN), F32),
            vm((rows, LN), F32),
            vm((rows, LN), F32),
            vm((rows, LN), F32),
            vm((cl, LN), F32),
            vm((rl, LN), F32),
            vm((cl, LN), F32),
            vm((cl, LN), F32),
            vm((rl, LN), F32),
            vm((ITERS, nc, rl, LN), F32),
            vm((ITERS, nr, cl, LN), F32),
            vm((nc, 8, LN), F32),
            vm((nr, 8, LN), F32),
            dma((ITERS, nc - 1)), dma((ITERS, nc - 1)),
            dma((ITERS, 2, nr - 1)), dma((ITERS, 2, nr - 1)),
            dma((nc - 1,)), dma((nc - 1,)),
            dma((nr - 1,)), dma((nr - 1,)),
        ],
        compiler_params=pltpu.CompilerParams(
            collective_id=0, has_side_effects=True, vmem_limit_bytes=60 * 1024 * 1024),
    )(treated.T, donors.T, treated_counts.reshape(rl, LN), donor_counts.reshape(cl, LN))
    return f.reshape(rows), g.reshape(cols)


def solution(mesh):
    in_specs = (P("row", None), P("col", None), P("row"), P("col"))
    out_specs = (P("row"), P("col"))
    return jax.shard_map(
        functools.partial(on_device, mesh.shape["row"], mesh.shape["col"]),
        mesh=mesh, in_specs=in_specs, out_specs=out_specs, check_vma=False,
    )
```

```python
import functools
import math

import jax
import jax.numpy as jnp
from jax import lax
from jax.experimental import pallas as pl
from jax.experimental.pallas import tpu as pltpu
from jax.sharding import PartitionSpec as P

ITERS = 4
LOG2E = math.log2(math.e)
LN2 = math.log(2.0)
CH = 1024
LN = 128
KS = CH // LN
RB = 256
RV = 128
SHIFT = 20.0
UR = 4
UC = 4
US = 4
MESH = pl.DeviceIdType.MESH
F32 = jnp.float32
BF16 = jnp.bfloat16


def split3(v):
    a = v.astype(BF16).astype(F32)
    r = v - a
    b = r.astype(BF16).astype(F32)
    return a, b, r - b


def kernel(nr, nc, x_ref, y_ref, tc_ref, dc_ref, f_ref, g_ref,
           xa, yt, e_ref, gam, m_ref, s_ref, om, q_ref, p_ref, u_ref, ysq, xsq,
           rbuf, cbuf, nbuf, mbuf, rs, rr, cs, cr, ns, nrv, ms, mr):
    dim, rows = x_ref.shape
    cols = y_ref.shape[1]
    nch = cols // CH
    nrb = rows // RB
    rl = rows // LN
    hrl = rl // 2
    cuts = (0, nch // 2, nch)
    me_r = lax.axis_index("row")
    me_c = lax.axis_index("col")
    row_peers = [lax.rem(me_r + d, nr) for d in range(1, nr)]
    col_peers = [lax.rem(me_c + d, nc) for d in range(1, nc)]

    barrier = pltpu.get_barrier_semaphore()
    for p in row_peers:
        pl.semaphore_signal(barrier, inc=1, device_id={"row": p}, device_id_type=MESH)
    for p in col_peers:
        pl.semaphore_signal(barrier, inc=1, device_id={"col": p}, device_id_type=MESH)

    def to_col(ref_at, send, recv):
        out = []
        for d, p in enumerate(col_peers):
            out.append(pltpu.make_async_remote_copy(
                src_ref=ref_at, dst_ref=ref_at, send_sem=send(d), recv_sem=recv(d),
                device_id={"col": p}, device_id_type=MESH))
        return out

    def to_row(ref_at, send, recv):
        out = []
        for d, p in enumerate(row_peers):
            out.append(pltpu.make_async_remote_copy(
                src_ref=ref_at, dst_ref=ref_at, send_sem=send(d), recv_sem=recv(d),
                device_id={"row": p}, device_id_type=MESH))
        return out

    tcf = tc_ref[...].astype(F32)
    dcf = dc_ref[...].astype(F32)
    xf = x_ref[...].astype(F32)
    c = xf * (4.0 * LOG2E)
    c1, c2, c3 = split3(c)
    ri = lax.broadcasted_iota(jnp.int32, (dim, 4 * dim), 0)
    ci = lax.broadcasted_iota(jnp.int32, (dim, 4 * dim), 1)
    wide = jnp.zeros((rows, 4 * dim), F32)
    for k, part in enumerate((c1, c2, c3)):
        place = (ri + k * dim == ci).astype(BF16)
        wide = wide + lax.dot_general(
            part.astype(BF16), place, (((0,), (0,)), ((), ())), preferred_element_type=F32)
    lane = lax.broadcasted_iota(jnp.int32, (rows, 4 * dim), 1)
    wide = jnp.where((lane >= 3 * dim) & (lane < 3 * dim + 3), 1.0, wide)
    xa[...] = wide.astype(BF16)
    sq = jnp.sum(xf * xf, axis=0, keepdims=True)
    for r in range(rl):
        xsq[r:r + 1, :] = sq[:, r * LN:(r + 1) * LN]

    def put_q(ch, q8):
        row = jnp.concatenate([q8[k:k + 1, :] for k in range(KS)], axis=1)
        a, b, cc = split3(row)
        r16 = lax.broadcasted_iota(jnp.int32, (16, CH), 0)
        val = jnp.where(r16 == 0, a, jnp.where(r16 == 1, b, jnp.where(r16 == 2, cc, jnp.where(r16 < 6, 1.0, 0.0))))
        yt[3 * dim:3 * dim + 16, pl.ds(pl.multiple_of(ch * CH, CH), CH)] = val.astype(BF16)

    def prep(ch, carry):
        js = pl.ds(pl.multiple_of(ch * CH, CH), CH)
        r8 = pl.ds(pl.multiple_of(ch * KS, KS), KS)
        yc = y_ref[:, js]
        for k in range(3):
            yt[k * dim:(k + 1) * dim, js] = yc
        yt[3 * dim + 16:4 * dim, js] = jnp.zeros((dim - 16, CH), BF16)
        t1 = yc.astype(F32)
        n2 = jnp.sum(t1 * t1, axis=0, keepdims=True)
        n8 = jnp.concatenate([n2[:, k * LN:(k + 1) * LN] for k in range(KS)], axis=0)
        ysq[r8, :] = n8
        q8 = jnp.log2(dc_ref[r8, :].astype(F32)) - (2.0 * LOG2E) * n8
        q_ref[r8, :] = q8
        put_q(ch, q8)
        return carry

    lax.fori_loop(0, nch, prep, 0)

    tsum = tcf[0:8, :]
    for r in range(1, rl // 8):
        tsum = tsum + tcf[r * 8:(r + 1) * 8, :]
    dsum = dcf[0:8, :]
    for r in range(1, cols // LN // 8):
        dsum = dsum + dcf[r * 8:(r + 1) * 8, :]
    mbuf[me_r] = tsum
    nbuf[me_c] = dsum

    pl.semaphore_wait(barrier, nr + nc - 2)
    n_copies = to_col(nbuf.at[me_c], lambda d: ns.at[d], lambda d: nrv.at[d])
    m_copies = to_row(mbuf.at[me_r], lambda d: ms.at[d], lambda d: mr.at[d])
    for cp in n_copies + m_copies:
        cp.start()

    def group(v, k):
        return v[:, k * LN:(k + 1) * LN]

    def score_rows(keep, before):
        m_ref[...] = jnp.full(m_ref.shape, -jnp.inf, F32)
        s_ref[...] = jnp.zeros(s_ref.shape, F32)

        def tile(step, carry):
            ch = step // nrb
            rb = step % nrb
            js = pl.ds(pl.multiple_of(ch * CH, CH), CH)
            rs_ = pl.ds(pl.multiple_of(rb * RB, RB), RB)
            sc = jnp.dot(xa[rs_, :], yt[:, js], preferred_element_type=F32)
            top = group(sc, 0)
            for k in range(1, KS):
                top = jnp.maximum(top, group(sc, k))
            old = m_ref[rs_, :]
            new = jnp.maximum(old, top)
            if keep:
                low = new - SHIFT
                gam[rs_, pl.ds(pl.multiple_of(ch * LN, LN), LN)] = new
            else:
                low = new
            tot = None
            for k in range(KS):
                ex = jnp.exp2(group(sc, k) - low)
                if keep:
                    e_ref[rs_, pl.ds(pl.multiple_of(ch * CH + k * LN, LN), LN)] = ex
                tot = ex if tot is None else tot + ex
            s_ref[rs_, :] = s_ref[rs_, :] * jnp.exp2(old - new) + tot
            m_ref[rs_, :] = new
            return carry

        for n in range(2):
            before(n)
            lax.fori_loop(cuts[n] * nrb, cuts[n + 1] * nrb, tile, 0, unroll=UR)

    def rows_dense_lse(it):
        for r in range(rl):
            mt = m_ref[r * LN:(r + 1) * LN, :].T
            st = s_ref[r * LN:(r + 1) * LN, :].T
            top = jnp.max(mt, axis=0, keepdims=True)
            tot = jnp.sum(st * jnp.exp2(mt - top), axis=0, keepdims=True)
            rbuf[it, me_c, r:r + 1, :] = top + jnp.log2(tot)

    def row_exchange(it):
        copies = to_col(rbuf.at[it, me_c], lambda d: rs.at[it, 0, d], lambda d: rr.at[it, 0, d])
        for cp in copies:
            cp.start()
        for cp in copies:
            cp.wait()

    def spread(v, r):
        return jnp.broadcast_to(v[r:r + 1, :], (LN, LN)).T

    def lse_merge(get, n):
        top = get(0)
        for k in range(1, n):
            top = jnp.maximum(top, get(k))
        tot = jnp.exp2(get(0) - top)
        for k in range(1, n):
            tot = tot + jnp.exp2(get(k) - top)
        return top + jnp.log2(tot)

    def sum_merge(get, n):
        tot = get(0)
        for k in range(1, n):
            tot = tot + get(k)
        return tot


    def col_copies(it, n):
        part = cbuf.at[it, me_r, cuts[n] * KS:cuts[n + 1] * KS]
        return to_row(part, lambda d: cs.at[it, n, d], lambda d: cr.at[it, n, d])

    def over_chunks(it, chunk):
        for n in range(2):
            lax.fori_loop(cuts[n], cuts[n + 1], chunk, 0)
            for cp in col_copies(it, n):
                cp.start()

    def wait_group(it, n):
        for cp in col_copies(it, n):
            cp.wait()

    score_rows(False, lambda n: None)
    rows_dense_lse(0)
    row_exchange(0)
    lsum = lse_merge(lambda k: rbuf[0, k], nc)
    p = jnp.log2(tcf) - lsum
    p_ref[...] = p
    l128 = lax.broadcasted_iota(jnp.int32, (LN, 2 * dim), 1)
    for r in range(rl):
        a, b, cc = split3(spread(p, r))
        half = xa[r * LN:(r + 1) * LN, 2 * dim:4 * dim].astype(F32)
        half = jnp.where(l128 == dim + 3, a, jnp.where(l128 == dim + 4, b, jnp.where(l128 == dim + 5, cc, half)))
        xa[r * LN:(r + 1) * LN, 2 * dim:4 * dim] = half.astype(BF16)

    def col_chunk(ch, carry):
        js = pl.ds(pl.multiple_of(ch * CH, CH), CH)

        def tile(rb, ms_):
            old, tot = ms_
            rs_ = pl.ds(pl.multiple_of(rb * RB, RB), RB)
            sc = jnp.dot(xa[rs_, :], yt[:, js], preferred_element_type=F32)
            sc = sc.reshape(RB // 8, 8, CH)
            new = jnp.maximum(old, jnp.max(sc, axis=0))
            ex = jnp.sum(jnp.exp2(sc - new[None]), axis=0)
            return new, tot * jnp.exp2(old - new) + ex

        top, tot = lax.fori_loop(
            0, nrb, tile, (jnp.full((8, CH), -jnp.inf, F32), jnp.zeros((8, CH), F32)), unroll=UC)
        best = jnp.max(top, axis=0, keepdims=True)
        tot = jnp.sum(tot * jnp.exp2(top - best), axis=0, keepdims=True)
        val = best + jnp.log2(tot)
        cbuf[0, me_r, pl.ds(pl.multiple_of(ch * KS, KS), KS), :] = jnp.concatenate(
            [group(val, k) for k in range(KS)], axis=0)
        return carry

    over_chunks(0, col_chunk)

    def new_q(ch, carry):
        r8 = pl.ds(pl.multiple_of(ch * KS, KS), KS)
        total = lse_merge(lambda k: cbuf[0, k, r8, :], nr)
        q8 = jnp.log2(dc_ref[r8, :].astype(F32)) + (q_ref[r8, :] - total)
        q_ref[r8, :] = q8
        put_q(ch, q8)
        return carry

    def take_q(n):
        wait_group(0, n)
        lax.fori_loop(cuts[n], cuts[n + 1], new_q, 0)

    score_rows(True, take_q)
    rows_dense_lse(1)
    row_exchange(1)
    lsum = lse_merge(lambda k: rbuf[1, k], nc) - SHIFT
    p_ref[...] = p_ref[...] - lsum
    for r in range(rl):
        rsl = slice(r * LN, (r + 1) * LN)
        lb = spread(lsum, r)
        for ch in range(nch):
            gam[rsl, ch * LN:(ch + 1) * LN] = jnp.exp2(gam[rsl, ch * LN:(ch + 1) * LN] + (SHIFT - lb))
        om[rsl, :] = spread(tcf, r)

    per = rows // RV // 2

    def half_copies(it, h):
        part = rbuf.at[it, me_c, h * hrl:(h + 1) * hrl]
        return to_col(part, lambda d: rs.at[it, h, d], lambda d: rr.at[it, h, d])

    def sum_cols(it, before):
        def chunk_of(h, ch):
            def tile(rv, acc):
                rs_ = pl.ds(pl.multiple_of(rv * RV, RV), RV)
                w = gam[rs_, pl.ds(pl.multiple_of(ch * LN, LN), LN)] * om[rs_, :]
                out = []
                for k in range(KS):
                    ex = e_ref[rs_, pl.ds(pl.multiple_of(ch * CH + k * LN, LN), LN)]
                    out.append(acc[k] + jnp.sum((ex * w).reshape(RV // 8, 8, LN), axis=0))
                return tuple(out)

            acc = lax.fori_loop(h * per, (h + 1) * per, tile, tuple(jnp.zeros((8, LN), F32) for _ in range(KS)), unroll=US)
            val = jnp.concatenate([jnp.sum(a, axis=0, keepdims=True) for a in acc], axis=0)
            return val * (2.0 ** (-2 * SHIFT))

        def first(ch, carry):
            cbuf[it, me_r, pl.ds(pl.multiple_of(ch * KS, KS), KS), :] = chunk_of(0, ch)
            return carry

        def second(ch, carry):
            r8 = pl.ds(pl.multiple_of(ch * KS, KS), KS)
            cbuf[it, me_r, r8, :] = cbuf[it, me_r, r8, :] + chunk_of(1, ch)
            return carry

        before(0)
        lax.fori_loop(0, nch, first, 0)
        before(1)
        over_chunks(it, second)

    def sum_rows(it):
        s_ref[...] = jnp.zeros(s_ref.shape, F32)

        def over(h, ch, carry):
            u8 = u_ref[pl.ds(pl.multiple_of(ch * KS, KS), KS), :]

            def tile(rv, carry2):
                rs_ = pl.ds(pl.multiple_of(rv * RV, RV), RV)
                tot = None
                for k in range(KS):
                    ex = e_ref[rs_, pl.ds(pl.multiple_of(ch * CH + k * LN, LN), LN)] * u8[k:k + 1, :]
                    tot = ex if tot is None else tot + ex
                s_ref[rs_, :] += tot * gam[rs_, pl.ds(pl.multiple_of(ch * LN, LN), LN)]
                return carry2

            return lax.fori_loop(h * per, (h + 1) * per, tile, carry, unroll=US)

        for n in range(2):
            wait_group(it - 1, n)
            sl = slice(cuts[n] * KS, cuts[n + 1] * KS)
            u_ref[sl, :] = dcf[sl, :] / sum_merge(lambda k: cbuf[it - 1, k, sl, :], nr)
            for h in range(2):
                lax.fori_loop(cuts[n], cuts[n + 1], functools.partial(over, h), 0)
                if n == 1:
                    for r in range(h * hrl, (h + 1) * hrl):
                        st = s_ref[r * LN:(r + 1) * LN, :].T
                        rbuf[it, me_c, r:r + 1, :] = jnp.sum(st, axis=0, keepdims=True) * (2.0 ** (-2 * SHIFT))
                    for cp in half_copies(it, h):
                        cp.start()

    sum_cols(1, lambda h: None)
    for it in range(2, ITERS):
        sum_rows(it)

        def weights(h, it=it):
            for cp in half_copies(it, h):
                cp.wait()
            sl = slice(h * hrl, (h + 1) * hrl)
            omega = tcf[sl, :] / sum_merge(lambda k: rbuf[it, k, sl, :], nc)
            for r in range(hrl):
                om[(h * hrl + r) * LN:(h * hrl + r + 1) * LN, :] = spread(omega, r)

        sum_cols(it, weights)
    for n in range(2):
        wait_group(ITERS - 1, n)
    total = sum_merge(lambda k: cbuf[ITERS - 1, k], nr)
    rsum = sum_merge(lambda k: rbuf[ITERS - 1, k], nc)

    for cp in n_copies + m_copies:
        cp.wait()
    mall = jnp.log2(jnp.sum(sum_merge(lambda k: mbuf[k], nr), keepdims=True))
    nall = jnp.log2(jnp.sum(sum_merge(lambda k: nbuf[k], nc), keepdims=True))
    f_ref[...] = (0.5 * LN2) * (
        p_ref[...] - jnp.log2(rsum) + ITERS * nall - (ITERS - 1) * mall) + xsq[...]
    g_ref[...] = (0.5 * LN2) * (
        q_ref[...] - jnp.log2(total) + ITERS * (mall - nall)) + ysq[...]


def on_device(nr, nc, treated, donors, treated_counts, donor_counts):
    rows, dim = treated.shape
    cols = donors.shape[0]
    rl, cl, nch = rows // LN, cols // LN, cols // CH
    vm = pltpu.VMEM
    dma = pltpu.SemaphoreType.DMA
    f, g = pl.pallas_call(
        functools.partial(kernel, nr, nc),
        out_shape=(jax.ShapeDtypeStruct((rl, LN), F32), jax.ShapeDtypeStruct((cl, LN), F32)),
        in_specs=[pl.BlockSpec(memory_space=vm)] * 4,
        out_specs=(pl.BlockSpec(memory_space=vm), pl.BlockSpec(memory_space=vm)),
        scratch_shapes=[
            vm((rows, 4 * dim), BF16),
            vm((4 * dim, cols), BF16),
            vm((rows, cols), F32),
            vm((rows, nch * LN), F32),
            vm((rows, LN), F32),
            vm((rows, LN), F32),
            vm((rows, LN), F32),
            vm((cl, LN), F32),
            vm((rl, LN), F32),
            vm((cl, LN), F32),
            vm((cl, LN), F32),
            vm((rl, LN), F32),
            vm((ITERS, nc, rl, LN), F32),
            vm((ITERS, nr, cl, LN), F32),
            vm((nc, 8, LN), F32),
            vm((nr, 8, LN), F32),
            dma((ITERS, 2, nc - 1)), dma((ITERS, 2, nc - 1)),
            dma((ITERS, 2, nr - 1)), dma((ITERS, 2, nr - 1)),
            dma((nc - 1,)), dma((nc - 1,)),
            dma((nr - 1,)), dma((nr - 1,)),
        ],
        compiler_params=pltpu.CompilerParams(
            collective_id=0, has_side_effects=True, vmem_limit_bytes=60 * 1024 * 1024),
    )(treated.T, donors.T, treated_counts.reshape(rl, LN), donor_counts.reshape(cl, LN))
    return f.reshape(rows), g.reshape(cols)


def solution(mesh):
    in_specs = (P("row", None), P("col", None), P("row"), P("col"))
    out_specs = (P("row"), P("col"))
    return jax.shard_map(
        functools.partial(on_device, mesh.shape["row"], mesh.shape["col"]),
        mesh=mesh, in_specs=in_specs, out_specs=out_specs, check_vma=False,
    )
```
